32 devices in a mesh: parts: 2 (over y), space: 4 (over z), dp: 2 (over x), chan: 2 (over core).
Axes of the slice: x: 2, y: 2, z: 4, core: 2. Of those that a mesh axis runs over, the one named last changes fastest.
Arguments:
- features: bfloat16 [4, 16, 64, 512], P(('parts', 'dp'), 'space'), parts along dimension 0, may hold values from -17 to 17
- cotangent: bfloat16 [4, 16, 64, 512], P(('parts', 'dp'), 'space', None, 'chan'), parts along dimension 0, may hold values from -6 to 6
- valid: int32 [4, 16, 64], P(('parts', 'dp'), 'space'), parts along dimension 0, may hold values from 0 to 1, as said below
- coefficients: bfloat16 [64, 8192], P(None, ('dp', 'chan')), may hold values from -0.046875 to 0.046875
Outputs:
- conv_out: bfloat16 [4, 16, 64, 512], P(('parts', 'dp'), 'space', None, 'chan'), parts along dimension 0
- input_grad: bfloat16 [4, 16, 64, 512], P(('parts', 'dp'), 'space', None, 'chan'), parts along dimension 0
- coef_grad: float32 [128, 8192], P(('parts', 'chan'), ('space', 'dp')), parts along dimension 0
The draws below stay inside these ranges and needn't reach their ends.
There are 2 independent parts, one for each index of `parts`. The reference program is written for one: setup_inputs(seed, part) draws one part's arguments, and reference() takes and returns one part's arrays. A program takes and returns all parts, laid end to end along the dimension named above; an argument that names none is the same for every part. Nothing has to cross between parts.
Inputs may be any that keep to these rules, and one draw needn't show every extreme that they name: `valid`: 1 marks a pixel whose loss counts.
All inputs are finite; a program needn't handle non-finite values.
Results may differ from the reference program's by a relative error of at most 0.009.
Values may be sent and summed in bfloat16 or wider, within the bound.
A program may use at most 128 MiB of HBM per device.

```python
import math
import jax
import jax.numpy as jnp
from jax import lax

FIELDS = 64
CHANNELS = 512
NB = 16
W = 64
CAMS = 2
H = 16


def draw_features(key, part):
    level = (jnp.arange(FIELDS * 8) // 8).astype(jnp.float32) / (FIELDS - 1)
    values = jnp.clip(jax.random.normal(key, (CAMS, H, W, FIELDS * 8), jnp.float32), -4.0, 4.0)
    return (values * jnp.power(3.0, level)).astype(jnp.bfloat16)


def draw_valid(key, part):
    low_key = jax.random.fold_in(key, 11)
    high_key = jax.random.fold_in(key, 12)
    pixel_key = jax.random.fold_in(key, 13)
    lower = jax.random.randint(low_key, (CAMS, 1, 1), 0, H // 4 + 1)
    upper = jax.random.randint(high_key, (CAMS, 1, 1), H - H // 4, H + 1)
    row_ids = jnp.arange(H).reshape(1, H, 1)
    pixel_bits = jax.random.randint(pixel_key, (CAMS, H, W), 0, 16)
    inside = (row_ids >= lower) & (row_ids < upper)
    return jnp.where(inside, pixel_bits < 14, pixel_bits < 1).astype(jnp.int32)


def steps_of(key, shape, pieces, smallest, top_value):
    loudness, own = 1.0, jax.random.fold_in(key, 6)
    for dim, parts in pieces:
        heights = jnp.exp(jax.random.uniform(jax.random.fold_in(own, dim), (parts,), jnp.float32, smallest / len(pieces), top_value / len(pieces)))
        loudness = loudness * jnp.repeat(heights, shape[dim] // parts).reshape([-1 if axis == dim else 1 for axis in range(len(shape))])
    return loudness


def normal_values(key, dims, scale, bound, split=(), kind=jnp.bfloat16):
    drawn = jax.random.normal(key, dims, jnp.float32) * scale
    if len(split) > 0:
        drawn = steps_of(key, dims, split, -0.22, 0.18) * drawn
    return jnp.clip(drawn, min=-bound, max=bound).astype(kind)


def setup_inputs(seed: int = 0, part: int = 0) -> dict:
    arg_keys = jax.random.split(jax.random.key(seed), 5)
    part_splits = jax.random.split(jax.random.fold_in(arg_keys[4], part), 5)
    return {
        "features": draw_features(jax.random.fold_in(jax.random.fold_in(arg_keys[4], part), 71), part),
        "cotangent": normal_values(part_splits[1], (CAMS, H, W, CHANNELS), 1.0, 6.0, ((0, 2), (1, 4), (3, 2))),
        "valid": draw_valid(jax.random.fold_in(jax.random.fold_in(arg_keys[4], part), 71), part),
        "coefficients": normal_values(arg_keys[3], (FIELDS, FIELDS * 8 * NB), (36 * CHANNELS) ** -0.5, 0.046875, ((1, 4),)),
    }


def basis_table():
    taps = jnp.arange(9)
    row_step = taps // 3 - 1
    col_step = taps % 3 - 1
    cycle = jnp.abs(row_step) + jnp.abs(col_step)
    angle = jnp.arctan2(row_step.astype(jnp.float32), col_step.astype(jnp.float32))
    turns = jnp.arange(8).astype(jnp.float32) * (2.0 * math.pi / 8.0)
    rotated = angle[:, None] - turns[None, :]
    cycle_of = jnp.array([0, 1, 1, 1, 1, 1, 1, 1, 1, 2, 2, 2, 2, 2, 2, 2], dtype=jnp.int32)
    freq = jnp.array([0, 0, 1, 1, 2, 2, 3, 3, 4, 0, 1, 1, 2, 2, 3, 3], dtype=jnp.float32)
    sine = jnp.array([0, 0, 0, 1, 0, 1, 0, 1, 0, 0, 0, 1, 0, 1, 0, 1], dtype=jnp.int32)
    phase = rotated[:, :, None] * freq[None, None, :]
    wave = jnp.where(sine[None, None, :] == 1, jnp.sin(phase), jnp.cos(phase))
    return jnp.where(cycle[:, None, None] == cycle_of[None, None, :], wave, jnp.zeros_like(wave))

def rotation_select():
    first = jnp.arange(8)[:, None, None]
    second = jnp.arange(8)[None, :, None]
    offset = jnp.arange(8)[None, None, :]
    return ((second - first) % 8 == offset).astype(jnp.float32)

def expand(panel, table, select):
    out_fields = panel.shape[0]
    in_fields = panel.shape[1] // (8 * NB)
    coeffs = panel.astype(jnp.float32).reshape(out_fields, in_fields, 8, NB)
    blocks = []
    for tap_index in range(9):
        mixed = jnp.einsum('abdn,in->iabd', coeffs, table[tap_index], precision=lax.Precision.HIGHEST)
        placed = jnp.einsum('iabd,ijd->aibj', mixed, select, precision=lax.Precision.HIGHEST)
        blocks.append(placed.reshape(out_fields * 8, in_fields * 8))
    return jnp.stack(blocks).astype(jnp.bfloat16)

def contract(gram, table_tap, select):
    out_fields = gram.shape[0] // 8
    in_fields = gram.shape[1] // 8
    blocks = gram.reshape(out_fields, 8, in_fields, 8)
    diagonal = jnp.einsum('aibj,ijd->abid', blocks, select, precision=lax.Precision.HIGHEST)
    return jnp.einsum('abid,in->abdn', diagonal, table_tap, precision=lax.Precision.HIGHEST)

def reference(features, cotangent, valid, coefficients):
    table = basis_table()
    select = rotation_select()
    kernel = expand(coefficients, table, select)
    cameras, frame_rows, frame_cols, channels = features.shape
    padded_x = jnp.pad(features, ((0, 0), (1, 1), (1, 1), (0, 0)))
    masked = cotangent * valid[..., None].astype(jnp.bfloat16)
    padded_g = jnp.pad(masked, ((0, 0), (1, 1), (1, 1), (0, 0)))
    masked_flat = masked.reshape(-1, channels)
    total_out = jnp.zeros((cameras * frame_rows * frame_cols, channels), jnp.float32)
    total_back = jnp.zeros((cameras * frame_rows * frame_cols, channels), jnp.float32)
    raw = jnp.zeros((FIELDS, FIELDS, 8, NB), jnp.float32)
    for tap_index in range(9):
        row_step = tap_index // 3 - 1
        col_step = tap_index % 3 - 1
        shifted_x = padded_x[:, 1 + row_step:1 + row_step + frame_rows, 1 + col_step:1 + col_step + frame_cols, :].reshape(-1, channels)
        shifted_g = padded_g[:, 1 - row_step:1 - row_step + frame_rows, 1 - col_step:1 - col_step + frame_cols, :].reshape(-1, channels)
        total_out = total_out + lax.dot_general(shifted_x, kernel[tap_index], (((1,), (1,)), ((), ())), preferred_element_type=jnp.float32)
        total_back = total_back + jnp.dot(shifted_g, kernel[tap_index], preferred_element_type=jnp.float32)
        gram = lax.dot_general(masked_flat, shifted_x, (((0,), (0,)), ((), ())), preferred_element_type=jnp.float32)
        raw = raw + contract(gram, table[tap_index], select)
    raw_flat = raw.reshape(FIELDS, FIELDS * 8 * NB)
    norm = jnp.sqrt(jnp.sum(raw_flat * raw_flat) + 1e-06)
    factor = math.sqrt(FIELDS * FIELDS * 8 * NB) / norm
    conv_out = total_out.astype(jnp.bfloat16).reshape(features.shape)
    input_grad = total_back.astype(jnp.bfloat16).reshape(features.shape)
    return (conv_out, input_grad, raw_flat * factor)
```

```python
import functools
import math

import jax
import jax.numpy as jnp
import numpy as np
from jax import lax
from jax.experimental import pallas as pl
from jax.experimental.pallas import tpu as pltpu
from jax.sharding import PartitionSpec as P

FIELDS = 64
NB = 16


def padded_2(array, sides, width):
    for axis, dim in sides:
        size, length = (lax.axis_size(axis), array.shape[dim])
        up = [(i, (i + 1) % size) for i in range(size - 1)]
        down = [(j, i) for i, j in up]
        last = lax.slice_in_dim(array, length - width, length, axis=dim)
        first = lax.slice_in_dim(array, 0, width, axis=dim)
        before = lax.ppermute(last, axis, up)
        after = lax.ppermute(first, axis, down)
        array = jnp.concatenate([before, array, after], axis=dim)
    return array


def basis_table():
    taps = jnp.arange(9)
    row_step = taps // 3 - 1
    col_step = taps % 3 - 1
    cycle = jnp.abs(row_step) + jnp.abs(col_step)
    angle = jnp.arctan2(row_step.astype(jnp.float32), col_step.astype(jnp.float32))
    turns = jnp.arange(8).astype(jnp.float32) * (2.0 * math.pi / 8.0)
    rotated = angle[:, None] - turns[None, :]
    cycle_of = jnp.array([0, 1, 1, 1, 1, 1, 1, 1, 1, 2, 2, 2, 2, 2, 2, 2], dtype=jnp.int32)
    freq = jnp.array([0, 0, 1, 1, 2, 2, 3, 3, 4, 0, 1, 1, 2, 2, 3, 3], dtype=jnp.float32)
    sine = jnp.array([0, 0, 0, 1, 0, 1, 0, 1, 0, 0, 0, 1, 0, 1, 0, 1], dtype=jnp.int32)
    phase = rotated[:, :, None] * freq[None, None, :]
    wave = jnp.where(sine[None, None, :] == 1, jnp.sin(phase), jnp.cos(phase))
    return jnp.where(cycle[:, None, None] == cycle_of[None, None, :], wave, jnp.zeros_like(wave))


def rotation_select():
    first = jnp.arange(8)[:, None, None]
    second = jnp.arange(8)[None, :, None]
    offset = jnp.arange(8)[None, None, :]
    return ((second - first) % 8 == offset).astype(jnp.float32)


def mixing_table(table, select):
    joined = table[:, :, None, None, :] * select[None, :, :, :, None]
    return joined.reshape(9, 64, 8 * NB)


def expand(panel, tap_mix):
    out_fields = panel.shape[0]
    in_fields = panel.shape[1] // (8 * NB)
    coeffs = panel.astype(jnp.float32).reshape(out_fields * in_fields, 8 * NB)
    blocks = []
    for tap_index in range(9):
        placed = lax.dot_general(
            coeffs,
            tap_mix[tap_index],
            (((1,), (1,)), ((), ())),
            precision=lax.Precision.HIGHEST,
            preferred_element_type=jnp.float32,
        )
        placed = placed.reshape(out_fields, in_fields, 8, 8).transpose(0, 2, 1, 3)
        blocks.append(placed.reshape(out_fields * 8, in_fields * 8).astype(jnp.bfloat16))
    return jnp.stack(blocks)


def contract(gram, mix_tap):
    out_fields = gram.shape[0] // 8
    in_fields = gram.shape[1] // 8
    blocks = (
        gram.reshape(out_fields, 8, in_fields, 8)
        .transpose(0, 2, 1, 3)
        .reshape(out_fields * in_fields, 64)
    )
    return jnp.dot(
        blocks, mix_tap, precision=lax.Precision.HIGHEST, preferred_element_type=jnp.float32
    )


def convolve(padded, kernel_taps, layout):
    shaped = kernel_taps.reshape(3, 3, kernel_taps.shape[1], kernel_taps.shape[2])
    return lax.conv_general_dilated(
        padded,
        shaped,
        (1, 1),
        ((0, 0), (1, 1)),
        dimension_numbers=("NHWC", layout, "NHWC"),
        preferred_element_type=jnp.float32,
    )


def local(features, cotangent, valid, coefficients):
    tap_mix = mixing_table(basis_table(), rotation_select())
    coef_all = lax.all_gather(coefficients, ("dp", "chan"), axis=1, tiled=True)
    share = FIELDS // lax.axis_size("chan")
    first_field = lax.axis_index("chan") * share
    own_rows = lax.dynamic_slice_in_dim(coef_all, first_field, share, 0)
    kernel_out = expand(own_rows, tap_mix)
    cameras, band_rows, frame_cols, channels = features.shape
    own_channels = share * 8
    masked = cotangent * valid[..., None].astype(jnp.bfloat16)
    stacked = jnp.concatenate([features, masked], axis=3)
    padded = padded_2(stacked, (("space", 1),), 1)
    padded_x = padded[..., :channels]
    padded_g = padded[..., channels:]
    total_out = convolve(padded_x, kernel_out, "HWOI")
    total_back = convolve(padded_g, kernel_out[::-1], "HWIO")
    gram_all = lax.conv_general_dilated(
        padded_x,
        masked,
        (1, 1),
        ((0, 0), (1, 1)),
        dimension_numbers=("CHWN", "IHWO", "NHWC"),
        preferred_element_type=jnp.float32,
    )
    gram_taps = gram_all.reshape(channels, 9, own_channels).transpose(1, 2, 0)
    raw = jnp.zeros((share * FIELDS, 8 * NB), jnp.float32)
    for tap_index in range(9):
        raw = raw + contract(gram_taps[tap_index], tap_mix[tap_index])
    summed = lax.psum_scatter(
        total_back.astype(jnp.bfloat16), "chan", scatter_dimension=3, tiled=True
    )
    raw_flat = raw.reshape(share, FIELDS * 8 * NB)
    shares = lax.psum_scatter(raw_flat, ("space", "dp"), scatter_dimension=1, tiled=True)
    squares = lax.psum(jnp.sum(shares * shares), ("space", "dp", "chan"))
    norm = jnp.sqrt(squares + 1e-06)
    factor = math.sqrt(FIELDS * FIELDS * 8 * NB) / norm
    conv_out = total_out.astype(jnp.bfloat16)
    return (conv_out, summed, shares * factor)


TURNS = (((0, 1), (1, 0), (0, -1), (-1, 0)), ((1, 1), (1, -1), (-1, -1), (-1, 1)))


def mixing_matrix():
    table = np.zeros((3, 8, 8, 8, NB))
    for cycle in range(3):
        for i in range(8):
            psi = 2.0 * math.pi * ((cycle == 2) - i) / 8.0
            waves = np.zeros(NB)
            if cycle == 0:
                waves[0] = 1.0
            else:
                full = [1.0]
                for freq in range(1, 5):
                    full += [math.cos(freq * psi), math.sin(freq * psi)]
                first = 1 if cycle == 1 else 9
                count = 8 if cycle == 1 else 7
                waves[first : first + count] = full[:count]
            for j in range(8):
                table[cycle, i, j, (j - i) % 8] = waves
    return table.reshape(192, 8 * NB).astype(np.float32)


def dot(a, b, dims):
    return lax.dot_general(a, b, ((dims[:1], dims[1:]), ((), ())), preferred_element_type=jnp.float32)


def grid_ids(rows, cols):
    return (
        lax.broadcasted_iota(jnp.int32, (rows, cols), 0),
        lax.broadcasted_iota(jnp.int32, (rows, cols), 1),
    )


def ones_at(cond):
    return jnp.where(cond, 1.0, 0.0).astype(jnp.bfloat16)


def lane_groups(pieces, shape):
    group = lax.broadcasted_iota(jnp.int32, shape, len(shape) - 1) // 32
    out = pieces[0]
    for k in range(1, 4):
        out = jnp.where(group == k, pieces[k], out)
    return out


def rolled(array, groups):
    if groups % 4 == 0:
        return array
    flat = array.reshape(-1, 128)
    return pltpu.roll(flat, 32 * (groups % 4), 1).reshape(array.shape)


def fused_kernel(
    sizes,
    x_ref, g_ref, v_ref, c_ref, mix_ref, mixt_ref,
    out_ref, back_ref, grad_ref,
    xp, mp, cg, xs, blocks, kt, back_own, back_send, back_recv,
    raw_send, raw_recv, sq_send, sq_recv,
    hs_sem, hr_sem, cs_sem, cr_sem, bs_sem, br_sem, rs_sem, rr_sem, ss_sem, sr_sem,
):
    n_space, n_dp, n_chan, rows, cols = sizes
    pix = rows * cols
    space, dp, chan = lax.axis_index("space"), lax.axis_index("dp"), lax.axis_index("chan")
    bf16 = jnp.bfloat16
    n_own = n_space * n_dp
    n_all = n_own * n_chan
    me_own = space * n_dp + dp
    me_all = me_own * n_chan + chan
    me_coef = dp * n_chan + chan
    n_coef = n_dp * n_chan

    def id_all(k):
        o = lax.rem(me_all + k, n_all)
        return {
            "space": o // (n_dp * n_chan),
            "dp": lax.rem(o // n_chan, n_dp),
            "chan": lax.rem(o, n_chan),
        }

    def send(src, dst, ssem, rsem, device):
        return pltpu.make_async_remote_copy(
            src_ref=src, dst_ref=dst, send_sem=ssem, recv_sem=rsem,
            device_id=device, device_id_type=pl.DeviceIdType.MESH,
        )

    barrier = pltpu.get_barrier_semaphore()
    for k in range(1, n_all):
        pl.semaphore_signal(barrier, inc=1, device_id=id_all(k), device_id_type=pl.DeviceIdType.MESH)

    r_id, c_id = grid_ids(256, 256)
    to_rot = ones_at(c_id == lax.rem(r_id, 8) * 32 + r_id // 8)
    r64, c64 = grid_ids(cols, cols)
    valid = v_ref[...].astype(jnp.float32)
    for r in range(rows):
        diag = jnp.where(r64 == c64, jnp.broadcast_to(valid[r : r + 1, :], (cols, cols)), 0.0).astype(bf16)
        row = dot(diag, g_ref[r * cols : (r + 1) * cols, :], (1, 0)).astype(bf16)
        mp[(r + 1) * cols : (r + 2) * cols, :] = dot(row, to_rot, (1, 0)).astype(bf16)

    @pl.when(space == 0)
    def _():
        xp[0:cols, :] = jnp.zeros((cols, 512), bf16)
        mp[0:cols, :] = jnp.zeros((cols, 256), bf16)

    @pl.when(space == n_space - 1)
    def _():
        xp[pix + cols : pix + 2 * cols, :] = jnp.zeros((cols, 512), bf16)
        mp[pix + cols : pix + 2 * cols, :] = jnp.zeros((cols, 256), bf16)

    pl.semaphore_wait(barrier, n_all - 1)

    down = {"space": lax.rem(space + 1, n_space)}
    up = {"space": lax.rem(space + n_space - 1, n_space)}
    lo, hi = pl.ds(0, cols), pl.ds(pix + cols, cols)
    last, first = pl.ds(pix, cols), pl.ds(cols, cols)
    x_down = send(x_ref.at[pl.ds(pix - cols, cols)], xp.at[lo], hs_sem.at[0], hr_sem.at[0], down)
    x_up = send(x_ref.at[pl.ds(0, cols)], xp.at[hi], hs_sem.at[1], hr_sem.at[1], up)
    m_down = send(mp.at[last], mp.at[lo], hs_sem.at[2], hr_sem.at[2], down)
    m_up = send(mp.at[first], mp.at[hi], hs_sem.at[3], hr_sem.at[3], up)

    @pl.when(space < n_space - 1)
    def _():
        x_down.start()
        m_down.start()

    @pl.when(space > 0)
    def _():
        x_up.start()
        m_up.start()

    coef_copies = []
    for k in range(1, n_coef):
        o = lax.rem(me_coef + k, n_coef)
        o_chan = lax.rem(o, n_chan)
        copy = send(
            c_ref.at[pl.ds(pl.multiple_of(o_chan * 32, 32), 32)], cg.at[me_coef],
            cs_sem.at[k], cr_sem.at[k], {"dp": o // n_chan, "chan": o_chan},
        )
        copy.start()
        coef_copies.append(copy)

    xp[cols : pix + cols, :] = x_ref[...]
    cg[me_coef] = c_ref[pl.ds(pl.multiple_of(chan * 32, 32), 32), :]
    shift_next = ones_at(c64 == r64 + 1)
    shift_prev = ones_at(c64 == r64 - 1)
    perms = [None] + [
        ones_at(r_id == (c_id // 8) * 8 + lax.rem(c_id + 2 * turn, 8)) for turn in (1, 2, 3)
    ]

    def wait_halo(a, b):
        @pl.when(space > 0)
        def _():
            a.wait_recv()

        @pl.when(space < n_space - 1)
        def _():
            b.wait_recv()

    wait_halo(x_down, x_up)

    def shifted(ref, row, dc):
        value = ref[row * cols : (row + 1) * cols, :]
        if dc == 0:
            return value
        return dot(shift_next if dc > 0 else shift_prev, value, (1, 0)).astype(bf16)

    for turn in range(4):
        for cycle in range(2):
            dr, dc = TURNS[cycle][turn]
            parts = [shifted(xp, 1 + r + dr, dc) for r in range(rows)]
            value = jnp.concatenate(parts, axis=0)
            for half in range(2):
                piece = value[:, half * 256 : (half + 1) * 256]
                if turn:
                    piece = dot(piece, perms[turn], (1, 0)).astype(bf16)
                xs[cycle, turn * pix : (turn + 1) * pix, half * 256 : (half + 1) * 256] = piece

    def turned(value, turn):
        if turn == 0:
            return value
        return jnp.concatenate([value[:, 64 * turn :], value[:, : 64 * turn]], axis=1)

    own_m = mp[cols : pix + cols, :]
    m_all = jnp.concatenate([turned(own_m, turn) for turn in range(4)], axis=0)
    for cycle in range(3):
        if cycle == 0:
            gram = dot(x_ref[...], own_m, (0, 0))
        else:
            gram = dot(xs[cycle - 1], m_all, (0, 0))
        for half in range(2):
            part = gram[:, half * 128 : (half + 1) * 128].reshape(16, 4, 8, 128)
            turns = [rolled(part, s) for s in range(4)]
            for q in range(4):
                place = lane_groups([turns[(k - q) % 4][:, k] for k in range(4)], (16, 8, 128))
                start = (cycle * 8 + half * 4 + q) * 8
                blocks[:, start : start + 8, :] = place
    per = 16 // n_own
    mixt = mixt_ref[...]
    for group in range(16):
        value = dot(mixt, blocks[group].astype(bf16), (1, 0))
        raw_send[group // per, group % per] = value.astype(bf16)
    raw_copies = []
    for k in range(1, n_own):
        o = lax.rem(me_own + k, n_own)
        copy = send(
            raw_send.at[o], raw_recv.at[me_own], rs_sem.at[k], rr_sem.at[k],
            {"space": o // n_dp, "dp": lax.rem(o, n_dp)},
        )
        copy.start()
        raw_copies.append(copy)
    raw_recv[me_own] = raw_send[me_own]

    for copy in coef_copies:
        copy.wait_recv()
    mix = mix_ref[...]
    per_slot = 64 // n_coef
    for group in range(16):
        stack = []
        for b in range(4 * group, 4 * group + 4):
            lane = (b % per_slot) * 128
            stack.append(cg[b // per_slot, :, lane : lane + 128])
        stack = jnp.concatenate(stack, axis=0)
        blocks[group] = dot(mix, jnp.concatenate([stack, stack], axis=1), (1, 1))
    for cycle in range(3):
        for half in range(2):
            source = []
            for q in range(4):
                start = (cycle * 8 + half * 4 + q) * 8
                part = blocks[:, start : start + 8, :]
                source.append([rolled(part, s) for s in range(4)])
            fields = [
                lane_groups([source[q][(q - k) % 4] for q in range(4)], (16, 8, 128)) for k in range(4)
            ]
            value = jnp.stack(fields, axis=1).reshape(512, 128).astype(bf16)
            kt[cycle, :, half * 128 : (half + 1) * 128] = value

    wait_halo(m_down, m_up)
    lane = lax.broadcasted_iota(jnp.int32, (pix, 512), 1)
    low = lax.rem(lane, 8) < 2
    total = None
    for turn in (3, 2, 1, 0):
        if total is not None:
            total = jnp.where(low, pltpu.roll(total, 512 - 6, 1), pltpu.roll(total, 2, 1))
        for cycle in range(2):
            dr, dc = TURNS[cycle][turn]
            parts = [shifted(mp, 1 + r - dr, -dc) for r in range(rows)]
            value = turned(jnp.concatenate(parts, axis=0), turn)
            term = dot(value, kt[cycle + 1], (1, 1))
            total = term if total is None else total + term
    total = total + dot(own_m, kt[0], (1, 1))
    left, right = total[:, :256], total[:, 256:]
    is_first = chan == 0
    back_own[...] = jnp.where(is_first, left, right)
    back_send[...] = jnp.where(is_first, right, left).astype(bf16)
    back_copy = send(back_send, back_recv, bs_sem, br_sem, {"chan": 1 - chan})
    back_copy.start()

    for copy in raw_copies:
        copy.wait_recv()
    summed = raw_recv[0].astype(jnp.float32)
    for k in range(1, n_own):
        summed = summed + raw_recv[k].astype(jnp.float32)
    sq_send[...] = jnp.sum((summed * summed).reshape(per * 16, 8, 128), axis=0)
    sq_copies = []
    for k in range(1, n_all):
        copy = send(sq_send, sq_recv.at[me_all], ss_sem.at[k], sr_sem.at[k], id_all(k))
        copy.start()
        sq_copies.append(copy)
    sq_recv[me_all] = sq_send[...]

    conv = dot(x_ref[...], kt[0], (1, 0))
    for turn in range(4):
        at = slice(turn * pix, (turn + 1) * pix)
        term = dot(xs[0, at, :], kt[1], (1, 0)) + dot(xs[1, at, :], kt[2], (1, 0))
        conv = conv + (pltpu.roll(term, 64 * turn, 1) if turn else term)
    out_ref[...] = dot(conv.astype(bf16), to_rot, (1, 1)).astype(bf16)

    back_copy.wait_recv()
    back_ref[...] = (back_own[...] + back_recv[...].astype(jnp.float32)).astype(bf16)

    flipped = [summed[g].T for g in range(per)]
    for copy in sq_copies:
        copy.wait_recv()
    squares = jnp.sum(jnp.sum(sq_recv[...], axis=0), keepdims=True)
    factor = math.sqrt(FIELDS * FIELDS * 8 * NB) / jnp.sqrt(squares + 1e-06)
    for b in range(4 * per):
        grad_ref[:, b * 128 : (b + 1) * 128] = flipped[b // 4][(b % 4) * 32 : (b % 4 + 1) * 32, :] * factor

    @pl.when(space < n_space - 1)
    def _():
        x_down.wait_send()
        m_down.wait_send()

    @pl.when(space > 0)
    def _():
        x_up.wait_send()
        m_up.wait_send()

    for copy in coef_copies + raw_copies + sq_copies + [back_copy]:
        copy.wait_send()


def fused(sizes, features, cotangent, valid, coefficients):
    n_space, n_dp, n_chan, rows, cols = sizes
    pix = rows * cols
    n_own, n_coef = n_space * n_dp, n_dp * n_chan
    n_all = n_own * n_chan
    per = 16 // n_own
    bf16, f32 = jnp.bfloat16, jnp.float32
    table = mixing_matrix()
    high = table.astype(bf16)
    low = (table - high.astype(np.float32)).astype(bf16)
    mix = jnp.asarray(np.concatenate([high, low], axis=1))
    mixt = jnp.asarray(np.ascontiguousarray(high.T))
    vmem = pl.BlockSpec(memory_space=pltpu.VMEM)
    dma = pltpu.SemaphoreType.DMA
    out, back, grad = pl.pallas_call(
        functools.partial(fused_kernel, sizes),
        out_shape=(
            jax.ShapeDtypeStruct((pix, 256), bf16),
            jax.ShapeDtypeStruct((pix, 256), bf16),
            jax.ShapeDtypeStruct((32, per * 512), f32),
        ),
        in_specs=[vmem] * 6,
        out_specs=[vmem] * 3,
        scratch_shapes=[
            pltpu.VMEM((pix + 2 * cols, 512), bf16),
            pltpu.VMEM((pix + 2 * cols, 256), bf16),
            pltpu.VMEM((n_coef, 32, coefficients.shape[1]), bf16),
            pltpu.VMEM((2, 4 * pix, 512), bf16),
            pltpu.VMEM((16, 192, 128), f32),
            pltpu.VMEM((3, 512, 256), bf16),
            pltpu.VMEM((pix, 256), f32),
            pltpu.VMEM((pix, 256), bf16),
            pltpu.VMEM((pix, 256), bf16),
            pltpu.VMEM((n_own, per, 128, 128), bf16),
            pltpu.VMEM((n_own, per, 128, 128), bf16),
            pltpu.VMEM((8, 128), f32),
            pltpu.VMEM((n_all, 8, 128), f32),
            dma((4,)), dma((4,)),
            dma((n_coef,)), dma((n_coef,)),
            dma, dma,
            dma((n_own,)), dma((n_own,)),
            dma((n_all,)), dma((n_all,)),
        ],
        compiler_params=pltpu.CompilerParams(
            collective_id=0, has_side_effects=True, vmem_limit_bytes=48 * 1024 * 1024
        ),
    )(
        features.reshape(pix, 512),
        cotangent.reshape(pix, 256),
        valid.reshape(rows, cols),
        coefficients,
        mix,
        mixt,
    )
    shape = (1, rows, cols, 256)
    return out.reshape(shape), back.reshape(shape), grad


def block(features, cotangent, valid, coefficients):
    n_space, n_dp, n_chan = (lax.axis_size(a) for a in ("space", "dp", "chan"))
    cameras, rows, cols, _ = features.shape
    owners = n_space * n_dp
    if cameras == 1 and n_chan == 2 and owners <= 16 and 16 % owners == 0 and cols % 16 == 0 and owners > 1:
        sizes = (n_space, n_dp, n_chan, rows, cols)
        return fused(sizes, features, cotangent, valid, coefficients)
    return local(features, cotangent, valid, coefficients)


def solution(mesh):
    in_specs = (
        P(("parts", "dp"), "space", None, None),
        P(("parts", "dp"), "space", None, "chan"),
        P(("parts", "dp"), "space", None),
        P(None, ("dp", "chan")),
    )
    out_specs = (
        P(("parts", "dp"), "space", None, "chan"),
        P(("parts", "dp"), "space", None, "chan"),
        P(("parts", "chan"), ("space", "dp")),
    )
    return jax.shard_map(block, mesh=mesh, in_specs=in_specs, out_specs=out_specs, check_vma=False)
```

```python
import functools
import math

import jax
import jax.numpy as jnp
import numpy as np
from jax import lax
from jax.experimental import pallas as pl
from jax.experimental.pallas import tpu as pltpu
from jax.sharding import PartitionSpec as P

FIELDS = 64
NB = 16


def padded_2(array, sides, width):
    for axis, dim in sides:
        size, length = (lax.axis_size(axis), array.shape[dim])
        up = [(i, (i + 1) % size) for i in range(size - 1)]
        down = [(j, i) for i, j in up]
        last = lax.slice_in_dim(array, length - width, length, axis=dim)
        first = lax.slice_in_dim(array, 0, width, axis=dim)
        before = lax.ppermute(last, axis, up)
        after = lax.ppermute(first, axis, down)
        array = jnp.concatenate([before, array, after], axis=dim)
    return array


def basis_table():
    taps = jnp.arange(9)
    row_step = taps // 3 - 1
    col_step = taps % 3 - 1
    cycle = jnp.abs(row_step) + jnp.abs(col_step)
    angle = jnp.arctan2(row_step.astype(jnp.float32), col_step.astype(jnp.float32))
    turns = jnp.arange(8).astype(jnp.float32) * (2.0 * math.pi / 8.0)
    rotated = angle[:, None] - turns[None, :]
    cycle_of = jnp.array([0, 1, 1, 1, 1, 1, 1, 1, 1, 2, 2, 2, 2, 2, 2, 2], dtype=jnp.int32)
    freq = jnp.array([0, 0, 1, 1, 2, 2, 3, 3, 4, 0, 1, 1, 2, 2, 3, 3], dtype=jnp.float32)
    sine = jnp.array([0, 0, 0, 1, 0, 1, 0, 1, 0, 0, 0, 1, 0, 1, 0, 1], dtype=jnp.int32)
    phase = rotated[:, :, None] * freq[None, None, :]
    wave = jnp.where(sine[None, None, :] == 1, jnp.sin(phase), jnp.cos(phase))
    return jnp.where(cycle[:, None, None] == cycle_of[None, None, :], wave, jnp.zeros_like(wave))


def rotation_select():
    first = jnp.arange(8)[:, None, None]
    second = jnp.arange(8)[None, :, None]
    offset = jnp.arange(8)[None, None, :]
    return ((second - first) % 8 == offset).astype(jnp.float32)


def mixing_table(table, select):
    joined = table[:, :, None, None, :] * select[None, :, :, :, None]
    return joined.reshape(9, 64, 8 * NB)


def expand(panel, tap_mix):
    out_fields = panel.shape[0]
    in_fields = panel.shape[1] // (8 * NB)
    coeffs = panel.astype(jnp.float32).reshape(out_fields * in_fields, 8 * NB)
    blocks = []
    for tap_index in range(9):
        placed = lax.dot_general(
            coeffs,
            tap_mix[tap_index],
            (((1,), (1,)), ((), ())),
            precision=lax.Precision.HIGHEST,
            preferred_element_type=jnp.float32,
        )
        placed = placed.reshape(out_fields, in_fields, 8, 8).transpose(0, 2, 1, 3)
        blocks.append(placed.reshape(out_fields * 8, in_fields * 8).astype(jnp.bfloat16))
    return jnp.stack(blocks)


def contract(gram, mix_tap):
    out_fields = gram.shape[0] // 8
    in_fields = gram.shape[1] // 8
    blocks = (
        gram.reshape(out_fields, 8, in_fields, 8)
        .transpose(0, 2, 1, 3)
        .reshape(out_fields * in_fields, 64)
    )
    return jnp.dot(
        blocks, mix_tap, precision=lax.Precision.HIGHEST, preferred_element_type=jnp.float32
    )


def convolve(padded, kernel_taps, layout):
    shaped = kernel_taps.reshape(3, 3, kernel_taps.shape[1], kernel_taps.shape[2])
    return lax.conv_general_dilated(
        padded,
        shaped,
        (1, 1),
        ((0, 0), (1, 1)),
        dimension_numbers=("NHWC", layout, "NHWC"),
        preferred_element_type=jnp.float32,
    )


def local(features, cotangent, valid, coefficients):
    tap_mix = mixing_table(basis_table(), rotation_select())
    coef_all = lax.all_gather(coefficients, ("dp", "chan"), axis=1, tiled=True)
    share = FIELDS // lax.axis_size("chan")
    first_field = lax.axis_index("chan") * share
    own_rows = lax.dynamic_slice_in_dim(coef_all, first_field, share, 0)
    kernel_out = expand(own_rows, tap_mix)
    cameras, band_rows, frame_cols, channels = features.shape
    own_channels = share * 8
    masked = cotangent * valid[..., None].astype(jnp.bfloat16)
    stacked = jnp.concatenate([features, masked], axis=3)
    padded = padded_2(stacked, (("space", 1),), 1)
    padded_x = padded[..., :channels]
    padded_g = padded[..., channels:]
    total_out = convolve(padded_x, kernel_out, "HWOI")
    total_back = convolve(padded_g, kernel_out[::-1], "HWIO")
    gram_all = lax.conv_general_dilated(
        padded_x,
        masked,
        (1, 1),
        ((0, 0), (1, 1)),
        dimension_numbers=("CHWN", "IHWO", "NHWC"),
        preferred_element_type=jnp.float32,
    )
    gram_taps = gram_all.reshape(channels, 9, own_channels).transpose(1, 2, 0)
    raw = jnp.zeros((share * FIELDS, 8 * NB), jnp.float32)
    for tap_index in range(9):
        raw = raw + contract(gram_taps[tap_index], tap_mix[tap_index])
    summed = lax.psum_scatter(
        total_back.astype(jnp.bfloat16), "chan", scatter_dimension=3, tiled=True
    )
    raw_flat = raw.reshape(share, FIELDS * 8 * NB)
    shares = lax.psum_scatter(raw_flat, ("space", "dp"), scatter_dimension=1, tiled=True)
    squares = lax.psum(jnp.sum(shares * shares), ("space", "dp", "chan"))
    norm = jnp.sqrt(squares + 1e-06)
    factor = math.sqrt(FIELDS * FIELDS * 8 * NB) / norm
    conv_out = total_out.astype(jnp.bfloat16)
    return (conv_out, summed, shares * factor)


TURNS = (((0, 1), (1, 0), (0, -1), (-1, 0)), ((1, 1), (1, -1), (-1, -1), (-1, 1)))


def mixing_matrix():
    table = np.zeros((3, 8, 8, 8, NB))
    for cycle in range(3):
        for i in range(8):
            psi = 2.0 * math.pi * ((cycle == 2) - i) / 8.0
            waves = np.zeros(NB)
            if cycle == 0:
                waves[0] = 1.0
            else:
                full = [1.0]
                for freq in range(1, 5):
                    full += [math.cos(freq * psi), math.sin(freq * psi)]
                first = 1 if cycle == 1 else 9
                count = 8 if cycle == 1 else 7
                waves[first : first + count] = full[:count]
            for j in range(8):
                table[cycle, i, j, (j - i) % 8] = waves
    return table.reshape(192, 8 * NB).astype(np.float32)


def dot(a, b, dims):
    return lax.dot_general(a, b, ((dims[:1], dims[1:]), ((), ())), preferred_element_type=jnp.float32)


def grid_ids(rows, cols):
    return (
        lax.broadcasted_iota(jnp.int32, (rows, cols), 0),
        lax.broadcasted_iota(jnp.int32, (rows, cols), 1),
    )


def ones_at(cond):
    return jnp.where(cond, 1.0, 0.0).astype(jnp.bfloat16)


def lane_groups(pieces, shape):
    group = lax.broadcasted_iota(jnp.int32, shape, len(shape) - 1) // 32
    out = pieces[0]
    for k in range(1, 4):
        out = jnp.where(group == k, pieces[k], out)
    return out


def rolled(array, groups):
    if groups % 4 == 0:
        return array
    flat = array.reshape(-1, 128)
    return pltpu.roll(flat, 32 * (groups % 4), 1).reshape(array.shape)


def fused_kernel(
    sizes,
    x_hbm, g_hbm, v_hbm, c_hbm, mix_hbm, mixt_hbm,
    out_ref, back_ref, grad_ref,
    xp, mp, cg, xs, blocks, kt, back_own, back_send, back_recv,
    raw_send, raw_recv, sq_send, sq_recv,
    g_ref, v_ref, c_ref, mix_ref, mixt_ref, in_sem,
    own_raw, z_send, z_recv, kblocks, ps_sem, pr_sem,
    hs_sem, hr_sem, cs_sem, cr_sem, bs_sem, br_sem, rs_sem, rr_sem, ss_sem, sr_sem,
):
    n_space, n_dp, n_chan, rows, cols = sizes
    pix = rows * cols
    space, dp, chan = lax.axis_index("space"), lax.axis_index("dp"), lax.axis_index("chan")
    bf16 = jnp.bfloat16
    n_own = n_space * n_dp
    n_all = n_own * n_chan
    me_own = space * n_dp + dp
    me_all = me_own * n_chan + chan
    me_coef = dp * n_chan + chan
    n_coef = n_dp * n_chan

    def step(index, k, size):
        moved = index + k
        return jnp.where(moved >= size, moved - size, moved)

    peers = [
        (ks, kd, kc)
        for ks in range(n_space)
        for kd in range(n_dp)
        for kc in range(n_chan)
        if ks or kd or kc
    ]

    def device(ks, kd, kc):
        return {"space": step(space, ks, n_space), "dp": step(dp, kd, n_dp), "chan": step(chan, kc, n_chan)}

    def send(src, dst, ssem, rsem, device):
        return pltpu.make_async_remote_copy(
            src_ref=src, dst_ref=dst, send_sem=ssem, recv_sem=rsem,
            device_id=device, device_id_type=pl.DeviceIdType.MESH,
        )

    loads = [
        pltpu.make_async_copy(src, dst, in_sem.at[k])
        for k, (src, dst) in enumerate(
            (
                (v_hbm, v_ref),
                (g_hbm, g_ref),
                (x_hbm, xp.at[pl.ds(cols, pix)]),
                (mixt_hbm, mixt_ref),
                (c_hbm.at[pl.ds(pl.multiple_of(chan * 32, 32), 32)], c_ref),
                (mix_hbm, mix_ref),
            )
        )
    ]
    for load in loads:
        load.start()

    barrier = pltpu.get_barrier_semaphore()
    for peer in peers:
        pl.semaphore_signal(
            barrier, inc=1, device_id=device(*peer), device_id_type=pl.DeviceIdType.MESH
        )

    r_id, c_id = grid_ids(256, 256)
    to_rot = ones_at(c_id == lax.rem(r_id, 8) * 32 + r_id // 8)
    r64, c64 = grid_ids(cols, cols)
    loads[0].wait()
    loads[1].wait()
    valid = v_ref[...].astype(jnp.float32)
    for r in range(rows):
        diag = jnp.where(r64 == c64, jnp.broadcast_to(valid[r : r + 1, :], (cols, cols)), 0.0).astype(bf16)
        row = dot(diag, g_ref[r * cols : (r + 1) * cols, :], (1, 0)).astype(bf16)
        mp[(r + 1) * cols : (r + 2) * cols, :] = dot(row, to_rot, (1, 0)).astype(bf16)

    @pl.when(space == 0)
    def _():
        xp[0:cols, :] = jnp.zeros((cols, 512), bf16)
        mp[0:cols, :] = jnp.zeros((cols, 256), bf16)

    @pl.when(space == n_space - 1)
    def _():
        xp[pix + cols : pix + 2 * cols, :] = jnp.zeros((cols, 512), bf16)
        mp[pix + cols : pix + 2 * cols, :] = jnp.zeros((cols, 256), bf16)

    pl.semaphore_wait(barrier, n_all - 1)

    down = {"space": step(space, 1, n_space)}
    up = {"space": step(space, n_space - 1, n_space)}
    lo, hi = pl.ds(0, cols), pl.ds(pix + cols, cols)
    last, first = pl.ds(pix, cols), pl.ds(cols, cols)
    x_down = send(x_hbm.at[pl.ds(pix - cols, cols)], xp.at[lo], hs_sem.at[0], hr_sem.at[0], down)
    x_up = send(x_hbm.at[pl.ds(0, cols)], xp.at[hi], hs_sem.at[1], hr_sem.at[1], up)
    m_down = send(mp.at[last], mp.at[lo], hs_sem.at[2], hr_sem.at[2], down)
    m_up = send(mp.at[first], mp.at[hi], hs_sem.at[3], hr_sem.at[3], up)

    @pl.when(space < n_space - 1)
    def _():
        x_down.start()
        m_down.start()

    @pl.when(space > 0)
    def _():
        x_up.start()
        m_up.start()

    coef_copies = []
    for k in range(1, n_coef):
        kd, kc = divmod(k, n_chan)
        o_chan = step(chan, kc, n_chan)
        copy = send(
            c_hbm.at[pl.ds(pl.multiple_of(o_chan * 32, 32), 32)], cg.at[me_coef],
            cs_sem.at[k], cr_sem.at[k], {"dp": step(dp, kd, n_dp), "chan": o_chan},
        )
        copy.start()
        coef_copies.append(copy)

    shift_next = ones_at(c64 == r64 + 1)
    shift_prev = ones_at(c64 == r64 - 1)
    perms = [None] + [
        ones_at(r_id == (c_id // 8) * 8 + lax.rem(c_id + 2 * turn, 8)) for turn in (1, 2, 3)
    ]

    def wait_halo(a, b):
        @pl.when(space > 0)
        def _():
            a.wait_recv()

        @pl.when(space < n_space - 1)
        def _():
            b.wait_recv()

    loads[2].wait()
    wait_halo(x_down, x_up)

    def shifted(ref, row, dc):
        value = ref[row * cols : (row + 1) * cols, :]
        if dc == 0:
            return value
        return dot(shift_next if dc > 0 else shift_prev, value, (1, 0)).astype(bf16)

    for turn in range(4):
        for cycle in range(2):
            dr, dc = TURNS[cycle][turn]
            parts = [shifted(xp, 1 + r + dr, dc) for r in range(rows)]
            value = jnp.concatenate(parts, axis=0)
            for half in range(2):
                piece = value[:, half * 256 : (half + 1) * 256]
                if turn:
                    piece = dot(piece, perms[turn], (1, 0)).astype(bf16)
                xs[cycle, turn * pix : (turn + 1) * pix, half * 256 : (half + 1) * 256] = piece

    def turned(value, turn):
        if turn == 0:
            return value
        return jnp.concatenate([value[:, 64 * turn :], value[:, : 64 * turn]], axis=1)

    own_m = mp[cols : pix + cols, :]
    m_all = jnp.concatenate([turned(own_m, turn) for turn in range(4)], axis=0)
    for cycle in range(3):
        if cycle == 0:
            gram = dot(xp[cols : pix + cols, :], own_m, (0, 0))
        else:
            gram = dot(xs[cycle - 1], m_all, (0, 0))
        for half in range(2):
            part = gram[:, half * 128 : (half + 1) * 128].reshape(16, 4, 8, 128)
            turns = [rolled(part, s) for s in range(4)]
            for q in range(4):
                place = lane_groups([turns[(k - q) % 4][:, k] for k in range(4)], (16, 8, 128))
                start = (cycle * 8 + half * 4 + q) * 8
                blocks[:, start : start + 8, :] = place
    per = 16 // n_own
    loads[3].wait()
    mixt = mixt_ref[...]

    def mixed(owner, g):
        return dot(mixt, blocks[owner * per + g].astype(bf16), (1, 0))

    order = sorted(range(n_space), key=lambda k: -min(k, n_space - k))
    dp_copies, raw_copies = [], []
    for ks in order:
        to_space = step(space, ks, n_space)
        for kd in range(1, n_dp):
            to_dp = step(dp, kd, n_dp)
            for g in range(per):
                raw_send[ks, kd, g] = mixed(to_space * n_dp + to_dp, g).astype(bf16)
            at = (ks, kd)
            copy = send(raw_send.at[at], raw_recv.at[at], ps_sem.at[at], pr_sem.at[at], {"dp": to_dp})
            copy.start()
            dp_copies.append((ks, copy))
    for ks in order:
        to_space = step(space, ks, n_space)
        for g in range(per):
            own_raw[ks, g] = mixed(to_space * n_dp + dp, g)

    loads[4].wait()
    loads[5].wait()
    cg[me_coef] = c_ref[...]
    for copy in coef_copies:
        copy.wait_recv()
    mix = mix_ref[...]
    per_slot = 64 // n_coef
    for group in range(16):
        stack = []
        for b in range(4 * group, 4 * group + 4):
            lane = (b % per_slot) * 128
            stack.append(cg[b // per_slot, :, lane : lane + 128])
        stack = jnp.concatenate(stack, axis=0)
        kblocks[group] = dot(mix, jnp.concatenate([stack, stack], axis=1), (1, 1))
    for ks in order:
        for at, copy in dp_copies:
            if at == ks:
                copy.wait_recv()
        value = own_raw[ks]
        for kd in range(1, n_dp):
            value = value + raw_recv[ks, kd].astype(jnp.float32)
        if ks == 0:
            own_raw[0] = value
        else:
            z_send[ks] = value.astype(bf16)
            copy = send(
                z_send.at[ks], z_recv.at[ks], rs_sem.at[ks], rr_sem.at[ks],
                {"space": step(space, ks, n_space)},
            )
            copy.start()
            raw_copies.append(copy)
    for cycle in range(3):
        for half in range(2):
            source = []
            for q in range(4):
                start = (cycle * 8 + half * 4 + q) * 8
                part = kblocks[:, start : start + 8, :]
                source.append([rolled(part, s) for s in range(4)])
            fields = [
                lane_groups([source[q][(q - k) % 4] for q in range(4)], (16, 8, 128)) for k in range(4)
            ]
            value = jnp.stack(fields, axis=1).reshape(512, 128).astype(bf16)
            kt[cycle, :, half * 128 : (half + 1) * 128] = value

    wait_halo(m_down, m_up)
    lane = lax.broadcasted_iota(jnp.int32, (pix, 512), 1)
    low = lax.rem(lane, 8) < 2
    total = None
    for turn in (3, 2, 1, 0):
        if total is not None:
            total = jnp.where(low, pltpu.roll(total, 512 - 6, 1), pltpu.roll(total, 2, 1))
        for cycle in range(2):
            dr, dc = TURNS[cycle][turn]
            parts = [shifted(mp, 1 + r - dr, -dc) for r in range(rows)]
            value = turned(jnp.concatenate(parts, axis=0), turn)
            term = dot(value, kt[cycle + 1], (1, 1))
            total = term if total is None else total + term
    total = total + dot(own_m, kt[0], (1, 1))
    left, right = total[:, :256], total[:, 256:]
    is_first = chan == 0
    back_own[...] = jnp.where(is_first, left, right)
    back_send[...] = jnp.where(is_first, right, left).astype(bf16)
    back_copy = send(back_send, back_recv, bs_sem, br_sem, {"chan": 1 - chan})
    back_copy.start()

    conv = dot(xp[cols : pix + cols, :], kt[0], (1, 0))
    for turn in range(4):
        at = slice(turn * pix, (turn + 1) * pix)
        term = dot(xs[0, at, :], kt[1], (1, 0)) + dot(xs[1, at, :], kt[2], (1, 0))
        conv = conv + (pltpu.roll(term, 64 * turn, 1) if turn else term)
    for copy in raw_copies:
        copy.wait_recv()
    summed = own_raw[0]
    for ks in range(1, n_space):
        summed = summed + z_recv[ks].astype(jnp.float32)
    sq_send[...] = jnp.sum((summed * summed).reshape(per * 16, 8, 128), axis=0)
    sq_copies = []
    for k, peer in enumerate(peers):
        copy = send(sq_send, sq_recv.at[me_all], ss_sem.at[k], sr_sem.at[k], device(*peer))
        copy.start()
        sq_copies.append(copy)
    sq_recv[me_all] = sq_send[...]

    out_ref[...] = dot(conv.astype(bf16), to_rot, (1, 1)).astype(bf16)

    back_copy.wait_recv()
    back_ref[...] = (back_own[...] + back_recv[...].astype(jnp.float32)).astype(bf16)

    flipped = [summed[g].T for g in range(per)]
    for copy in sq_copies:
        copy.wait_recv()
    squares = jnp.sum(jnp.sum(sq_recv[...], axis=0), keepdims=True)
    factor = math.sqrt(FIELDS * FIELDS * 8 * NB) / jnp.sqrt(squares + 1e-06)
    for b in range(4 * per):
        grad_ref[:, b * 128 : (b + 1) * 128] = flipped[b // 4][(b % 4) * 32 : (b % 4 + 1) * 32, :] * factor

    @pl.when(space < n_space - 1)
    def _():
        x_down.wait_send()
        m_down.wait_send()

    @pl.when(space > 0)
    def _():
        x_up.wait_send()
        m_up.wait_send()

    for copy in coef_copies + [c for _, c in dp_copies] + raw_copies + sq_copies + [back_copy]:
        copy.wait_send()


def fused(sizes, features, cotangent, valid, coefficients):
    n_space, n_dp, n_chan, rows, cols = sizes
    pix = rows * cols
    n_own, n_coef = n_space * n_dp, n_dp * n_chan
    n_all = n_own * n_chan
    per = 16 // n_own
    bf16, f32 = jnp.bfloat16, jnp.float32
    table = mixing_matrix()
    high = table.astype(bf16)
    low = (table - high.astype(np.float32)).astype(bf16)
    mix = jnp.asarray(np.concatenate([high, low], axis=1))
    mixt = jnp.asarray(np.ascontiguousarray(high.T))
    vmem = pl.BlockSpec(memory_space=pltpu.VMEM)
    dma = pltpu.SemaphoreType.DMA
    out, back, grad = pl.pallas_call(
        functools.partial(fused_kernel, sizes),
        out_shape=(
            jax.ShapeDtypeStruct((pix, 256), bf16),
            jax.ShapeDtypeStruct((pix, 256), bf16),
            jax.ShapeDtypeStruct((32, per * 512), f32),
        ),
        in_specs=[pl.BlockSpec(memory_space=pltpu.HBM)] * 6,
        out_specs=[vmem] * 3,
        scratch_shapes=[
            pltpu.VMEM((pix + 2 * cols, 512), bf16),
            pltpu.VMEM((pix + 2 * cols, 256), bf16),
            pltpu.VMEM((n_coef, 32, coefficients.shape[1]), bf16),
            pltpu.VMEM((2, 4 * pix, 512), bf16),
            pltpu.VMEM((16, 192, 128), f32),
            pltpu.VMEM((3, 512, 256), bf16),
            pltpu.VMEM((pix, 256), f32),
            pltpu.VMEM((pix, 256), bf16),
            pltpu.VMEM((pix, 256), bf16),
            pltpu.VMEM((n_space, n_dp, per, 128, 128), bf16),
            pltpu.VMEM((n_space, n_dp, per, 128, 128), bf16),
            pltpu.VMEM((8, 128), f32),
            pltpu.VMEM((n_all, 8, 128), f32),
            pltpu.VMEM((pix, 256), bf16),
            pltpu.VMEM((rows, cols), jnp.int32),
            pltpu.VMEM((32, coefficients.shape[1]), bf16),
            pltpu.VMEM(mix.shape, bf16),
            pltpu.VMEM(mixt.shape, bf16),
            dma((6,)),
            pltpu.VMEM((n_space, per, 128, 128), f32),
            pltpu.VMEM((n_space, per, 128, 128), bf16),
            pltpu.VMEM((n_space, per, 128, 128), bf16),
            pltpu.VMEM((16, 192, 128), f32),
            dma((n_space, n_dp)), dma((n_space, n_dp)),
            dma((4,)), dma((4,)),
            dma((n_coef,)), dma((n_coef,)),
            dma, dma,
            dma((n_space,)), dma((n_space,)),
            dma((n_all,)), dma((n_all,)),
        ],
        compiler_params=pltpu.CompilerParams(
            collective_id=0, has_side_effects=True, vmem_limit_bytes=63 * 1024 * 1024
        ),
    )(
        features.reshape(pix, 512),
        cotangent.reshape(pix, 256),
        valid.reshape(rows, cols),
        coefficients,
        mix,
        mixt,
    )
    shape = (1, rows, cols, 256)
    return out.reshape(shape), back.reshape(shape), grad


def block(features, cotangent, valid, coefficients):
    n_space, n_dp, n_chan = (lax.axis_size(a) for a in ("space", "dp", "chan"))
    cameras, rows, cols, _ = features.shape
    owners = n_space * n_dp
    if cameras == 1 and n_chan == 2 and owners <= 16 and 16 % owners == 0 and cols % 16 == 0 and owners > 1:
        sizes = (n_space, n_dp, n_chan, rows, cols)
        return fused(sizes, features, cotangent, valid, coefficients)
    return local(features, cotangent, valid, coefficients)


def solution(mesh):
    in_specs = (
        P(("parts", "dp"), "space", None, None),
        P(("parts", "dp"), "space", None, "chan"),
        P(("parts", "dp"), "space", None),
        P(None, ("dp", "chan")),
    )
    out_specs = (
        P(("parts", "dp"), "space", None, "chan"),
        P(("parts", "dp"), "space", None, "chan"),
        P(("parts", "chan"), ("space", "dp")),
    )
    return jax.shard_map(block, mesh=mesh, in_specs=in_specs, out_specs=out_specs, check_vma=False)
```

```python
import functools
import math

import jax
import jax.numpy as jnp
import numpy as np
from jax import lax
from jax.experimental import pallas as pl
from jax.experimental.pallas import tpu as pltpu
from jax.sharding import PartitionSpec as P

FIELDS = 64
NB = 16


def padded_2(array, sides, width):
    for axis, dim in sides:
        size, length = (lax.axis_size(axis), array.shape[dim])
        up = [(i, (i + 1) % size) for i in range(size - 1)]
        down = [(j, i) for i, j in up]
        last = lax.slice_in_dim(array, length - width, length, axis=dim)
        first = lax.slice_in_dim(array, 0, width, axis=dim)
        before = lax.ppermute(last, axis, up)
        after = lax.ppermute(first, axis, down)
        array = jnp.concatenate([before, array, after], axis=dim)
    return array


def basis_table():
    taps = jnp.arange(9)
    row_step = taps // 3 - 1
    col_step = taps % 3 - 1
    cycle = jnp.abs(row_step) + jnp.abs(col_step)
    angle = jnp.arctan2(row_step.astype(jnp.float32), col_step.astype(jnp.float32))
    turns = jnp.arange(8).astype(jnp.float32) * (2.0 * math.pi / 8.0)
    rotated = angle[:, None] - turns[None, :]
    cycle_of = jnp.array([0, 1, 1, 1, 1, 1, 1, 1, 1, 2, 2, 2, 2, 2, 2, 2], dtype=jnp.int32)
    freq = jnp.array([0, 0, 1, 1, 2, 2, 3, 3, 4, 0, 1, 1, 2, 2, 3, 3], dtype=jnp.float32)
    sine = jnp.array([0, 0, 0, 1, 0, 1, 0, 1, 0, 0, 0, 1, 0, 1, 0, 1], dtype=jnp.int32)
    phase = rotated[:, :, None] * freq[None, None, :]
    wave = jnp.where(sine[None, None, :] == 1, jnp.sin(phase), jnp.cos(phase))
    return jnp.where(cycle[:, None, None] == cycle_of[None, None, :], wave, jnp.zeros_like(wave))


def rotation_select():
    first = jnp.arange(8)[:, None, None]
    second = jnp.arange(8)[None, :, None]
    offset = jnp.arange(8)[None, None, :]
    return ((second - first) % 8 == offset).astype(jnp.float32)


def mixing_table(table, select):
    joined = table[:, :, None, None, :] * select[None, :, :, :, None]
    return joined.reshape(9, 64, 8 * NB)


def expand(panel, tap_mix):
    out_fields = panel.shape[0]
    in_fields = panel.shape[1] // (8 * NB)
    coeffs = panel.astype(jnp.float32).reshape(out_fields * in_fields, 8 * NB)
    blocks = []
    for tap_index in range(9):
        placed = lax.dot_general(
            coeffs,
            tap_mix[tap_index],
            (((1,), (1,)), ((), ())),
            precision=lax.Precision.HIGHEST,
            preferred_element_type=jnp.float32,
        )
        placed = placed.reshape(out_fields, in_fields, 8, 8).transpose(0, 2, 1, 3)
        blocks.append(placed.reshape(out_fields * 8, in_fields * 8).astype(jnp.bfloat16))
    return jnp.stack(blocks)


def contract(gram, mix_tap):
    out_fields = gram.shape[0] // 8
    in_fields = gram.shape[1] // 8
    blocks = (
        gram.reshape(out_fields, 8, in_fields, 8)
        .transpose(0, 2, 1, 3)
        .reshape(out_fields * in_fields, 64)
    )
    return jnp.dot(
        blocks, mix_tap, precision=lax.Precision.HIGHEST, preferred_element_type=jnp.float32
    )


def convolve(padded, kernel_taps, layout):
    shaped = kernel_taps.reshape(3, 3, kernel_taps.shape[1], kernel_taps.shape[2])
    return lax.conv_general_dilated(
        padded,
        shaped,
        (1, 1),
        ((0, 0), (1, 1)),
        dimension_numbers=("NHWC", layout, "NHWC"),
        preferred_element_type=jnp.float32,
    )


def local(features, cotangent, valid, coefficients):
    tap_mix = mixing_table(basis_table(), rotation_select())
    coef_all = lax.all_gather(coefficients, ("dp", "chan"), axis=1, tiled=True)
    share = FIELDS // lax.axis_size("chan")
    first_field = lax.axis_index("chan") * share
    own_rows = lax.dynamic_slice_in_dim(coef_all, first_field, share, 0)
    kernel_out = expand(own_rows, tap_mix)
    cameras, band_rows, frame_cols, channels = features.shape
    own_channels = share * 8
    masked = cotangent * valid[..., None].astype(jnp.bfloat16)
    stacked = jnp.concatenate([features, masked], axis=3)
    padded = padded_2(stacked, (("space", 1),), 1)
    padded_x = padded[..., :channels]
    padded_g = padded[..., channels:]
    total_out = convolve(padded_x, kernel_out, "HWOI")
    total_back = convolve(padded_g, kernel_out[::-1], "HWIO")
    gram_all = lax.conv_general_dilated(
        padded_x,
        masked,
        (1, 1),
        ((0, 0), (1, 1)),
        dimension_numbers=("CHWN", "IHWO", "NHWC"),
        preferred_element_type=jnp.float32,
    )
    gram_taps = gram_all.reshape(channels, 9, own_channels).transpose(1, 2, 0)
    raw = jnp.zeros((share * FIELDS, 8 * NB), jnp.float32)
    for tap_index in range(9):
        raw = raw + contract(gram_taps[tap_index], tap_mix[tap_index])
    summed = lax.psum_scatter(
        total_back.astype(jnp.bfloat16), "chan", scatter_dimension=3, tiled=True
    )
    raw_flat = raw.reshape(share, FIELDS * 8 * NB)
    shares = lax.psum_scatter(raw_flat, ("space", "dp"), scatter_dimension=1, tiled=True)
    squares = lax.psum(jnp.sum(shares * shares), ("space", "dp", "chan"))
    norm = jnp.sqrt(squares + 1e-06)
    factor = math.sqrt(FIELDS * FIELDS * 8 * NB) / norm
    conv_out = total_out.astype(jnp.bfloat16)
    return (conv_out, summed, shares * factor)


TURNS = (((0, 1), (1, 0), (0, -1), (-1, 0)), ((1, 1), (1, -1), (-1, -1), (-1, 1)))


def mixing_matrix():
    table = np.zeros((3, 8, 8, 8, NB))
    for cycle in range(3):
        for i in range(8):
            psi = 2.0 * math.pi * ((cycle == 2) - i) / 8.0
            waves = np.zeros(NB)
            if cycle == 0:
                waves[0] = 1.0
            else:
                full = [1.0]
                for freq in range(1, 5):
                    full += [math.cos(freq * psi), math.sin(freq * psi)]
                first = 1 if cycle == 1 else 9
                count = 8 if cycle == 1 else 7
                waves[first : first + count] = full[:count]
            for j in range(8):
                table[cycle, i, j, (j - i) % 8] = waves
    return table.reshape(192, 8 * NB).astype(np.float32)


def dot(a, b, dims):
    return lax.dot_general(a, b, ((dims[:1], dims[1:]), ((), ())), preferred_element_type=jnp.float32)


def grid_ids(rows, cols):
    return (
        lax.broadcasted_iota(jnp.int32, (rows, cols), 0),
        lax.broadcasted_iota(jnp.int32, (rows, cols), 1),
    )


def ones_at(cond):
    return jnp.where(cond, 1.0, 0.0).astype(jnp.bfloat16)


def lane_groups(pieces, shape):
    group = lax.broadcasted_iota(jnp.int32, shape, len(shape) - 1) // 32
    out = pieces[0]
    for k in range(1, 4):
        out = jnp.where(group == k, pieces[k], out)
    return out


def rolled(array, groups):
    if groups % 4 == 0:
        return array
    flat = array.reshape(-1, 128)
    return pltpu.roll(flat, 32 * (groups % 4), 1).reshape(array.shape)


def fused_kernel(
    sizes,
    x_hbm, g_hbm, v_hbm, c_hbm, mix_hbm, mixt_hbm,
    out_ref, back_ref, grad_ref,
    xp, mp, cg, xs, blocks, kt, back_own, back_send, back_recv,
    raw_send, raw_recv, sq_send, sq_recv,
    g_ref, v_ref, c_ref, mix_ref, mixt_ref, in_sem,
    own_raw, z_send, z_recv, kblocks, ps_sem, pr_sem,
    hs_sem, hr_sem, cs_sem, cr_sem, bs_sem, br_sem, rs_sem, rr_sem, ss_sem, sr_sem,
):
    n_space, n_dp, n_chan, rows, cols = sizes
    pix = rows * cols
    space, dp, chan = lax.axis_index("space"), lax.axis_index("dp"), lax.axis_index("chan")
    bf16 = jnp.bfloat16
    n_own = n_space * n_dp
    n_all = n_own * n_chan
    me_own = space * n_dp + dp
    me_all = me_own * n_chan + chan
    me_coef = dp * n_chan + chan
    n_coef = n_dp * n_chan

    def step(index, k, size):
        moved = index + k
        return jnp.where(moved >= size, moved - size, moved)

    peers = [
        (ks, kd, kc)
        for ks in range(n_space)
        for kd in range(n_dp)
        for kc in range(n_chan)
        if ks or kd or kc
    ]

    def device(ks, kd, kc):
        return {"space": step(space, ks, n_space), "dp": step(dp, kd, n_dp), "chan": step(chan, kc, n_chan)}

    def send(src, dst, ssem, rsem, device):
        return pltpu.make_async_remote_copy(
            src_ref=src, dst_ref=dst, send_sem=ssem, recv_sem=rsem,
            device_id=device, device_id_type=pl.DeviceIdType.MESH,
        )

    loads = [
        pltpu.make_async_copy(src, dst, in_sem.at[k])
        for k, (src, dst) in enumerate(
            (
                (v_hbm, v_ref),
                (g_hbm, g_ref),
                (x_hbm, xp.at[pl.ds(cols, pix)]),
                (mixt_hbm, mixt_ref),
                (c_hbm.at[pl.ds(pl.multiple_of(chan * 32, 32), 32)], c_ref),
                (mix_hbm, mix_ref),
            )
        )
    ]
    for load in loads:
        load.start()

    barrier = pltpu.get_barrier_semaphore()
    for peer in peers:
        pl.semaphore_signal(
            barrier, inc=1, device_id=device(*peer), device_id_type=pl.DeviceIdType.MESH
        )

    r_id, c_id = grid_ids(256, 256)
    to_rot = ones_at(c_id == lax.rem(r_id, 8) * 32 + r_id // 8)
    r64, c64 = grid_ids(cols, cols)
    loads[0].wait()
    loads[1].wait()
    valid = v_ref[...].astype(jnp.float32)
    for r in range(rows):
        diag = jnp.where(r64 == c64, jnp.broadcast_to(valid[r : r + 1, :], (cols, cols)), 0.0).astype(bf16)
        row = dot(diag, g_ref[r * cols : (r + 1) * cols, :], (1, 0)).astype(bf16)
        mp[(r + 1) * cols : (r + 2) * cols, :] = dot(row, to_rot, (1, 0)).astype(bf16)

    @pl.when(space == 0)
    def _():
        xp[0:cols, :] = jnp.zeros((cols, 512), bf16)
        mp[0:cols, :] = jnp.zeros((cols, 256), bf16)

    @pl.when(space == n_space - 1)
    def _():
        xp[pix + cols : pix + 2 * cols, :] = jnp.zeros((cols, 512), bf16)
        mp[pix + cols : pix + 2 * cols, :] = jnp.zeros((cols, 256), bf16)

    pl.semaphore_wait(barrier, n_all - 1)

    down = {"space": step(space, 1, n_space)}
    up = {"space": step(space, n_space - 1, n_space)}
    lo, hi = pl.ds(0, cols), pl.ds(pix + cols, cols)
    last, first = pl.ds(pix, cols), pl.ds(cols, cols)
    x_down = send(x_hbm.at[pl.ds(pix - cols, cols)], xp.at[lo], hs_sem.at[0], hr_sem.at[0], down)
    x_up = send(x_hbm.at[pl.ds(0, cols)], xp.at[hi], hs_sem.at[1], hr_sem.at[1], up)
    m_down = send(mp.at[last], mp.at[lo], hs_sem.at[2], hr_sem.at[2], down)
    m_up = send(mp.at[first], mp.at[hi], hs_sem.at[3], hr_sem.at[3], up)

    @pl.when(space < n_space - 1)
    def _():
        x_down.start()
        m_down.start()

    @pl.when(space > 0)
    def _():
        x_up.start()
        m_up.start()

    coef_copies = []
    for k in range(1, n_coef):
        kd, kc = divmod(k, n_chan)
        o_chan = step(chan, kc, n_chan)
        copy = send(
            c_hbm.at[pl.ds(pl.multiple_of(o_chan * 32, 32), 32)], cg.at[me_coef],
            cs_sem.at[k], cr_sem.at[k], {"dp": step(dp, kd, n_dp), "chan": o_chan},
        )
        copy.start()
        coef_copies.append(copy)

    shift_next = ones_at(c64 == r64 + 1)
    shift_prev = ones_at(c64 == r64 - 1)
    perms = [None] + [
        ones_at(r_id == (c_id // 8) * 8 + lax.rem(c_id + 2 * turn, 8)) for turn in (1, 2, 3)
    ]

    def wait_halo(a, b):
        @pl.when(space > 0)
        def _():
            a.wait_recv()

        @pl.when(space < n_space - 1)
        def _():
            b.wait_recv()

    loads[2].wait()
    wait_halo(x_down, x_up)

    def shifted(ref, row, dc):
        value = ref[row * cols : (row + 1) * cols, :]
        if dc == 0:
            return value
        return dot(shift_next if dc > 0 else shift_prev, value, (1, 0)).astype(bf16)

    for turn in range(4):
        for cycle in range(2):
            dr, dc = TURNS[cycle][turn]
            parts = [shifted(xp, 1 + r + dr, dc) for r in range(rows)]
            value = jnp.concatenate(parts, axis=0)
            for half in range(2):
                piece = value[:, half * 256 : (half + 1) * 256]
                if turn:
                    piece = dot(piece, perms[turn], (1, 0)).astype(bf16)
                xs[cycle, turn * pix : (turn + 1) * pix, half * 256 : (half + 1) * 256] = piece

    def turned(value, turn):
        if turn == 0:
            return value
        return jnp.concatenate([value[:, 64 * turn :], value[:, : 64 * turn]], axis=1)

    own_m = mp[cols : pix + cols, :]
    m_all = jnp.concatenate([turned(own_m, turn) for turn in range(4)], axis=0)
    for cycle in range(3):
        if cycle == 0:
            gram = dot(xp[cols : pix + cols, :], own_m, (0, 0))
        else:
            gram = dot(xs[cycle - 1], m_all, (0, 0))
        for half in range(2):
            part = gram[:, half * 128 : (half + 1) * 128].reshape(16, 4, 8, 128)
            turns = [rolled(part, s) for s in range(4)]
            for q in range(4):
                place = lane_groups([turns[(k - q) % 4][:, k] for k in range(4)], (16, 8, 128))
                start = (cycle * 8 + half * 4 + q) * 8
                blocks[:, start : start + 8, :] = place
    per = 16 // n_own
    loads[3].wait()
    mixt = mixt_ref[...]

    def mixed(owner, g):
        return dot(mixt, blocks[owner * per + g].astype(bf16), (1, 0))

    order = sorted(range(n_space), key=lambda k: -min(k, n_space - k))
    dp_copies, raw_copies = [], []
    for ks in order:
        to_space = step(space, ks, n_space)
        for kd in range(1, n_dp):
            to_dp = step(dp, kd, n_dp)
            for g in range(per):
                raw_send[ks, kd, g] = mixed(to_space * n_dp + to_dp, g).astype(bf16)
            at = (ks, kd)
            copy = send(raw_send.at[at], raw_recv.at[at], ps_sem.at[at], pr_sem.at[at], {"dp": to_dp})
            copy.start()
            dp_copies.append((ks, copy))
    for ks in order:
        to_space = step(space, ks, n_space)
        for g in range(per):
            own_raw[ks, g] = mixed(to_space * n_dp + dp, g)

    loads[4].wait()
    loads[5].wait()
    cg[me_coef] = c_ref[...]
    for copy in coef_copies:
        copy.wait_recv()
    mix = mix_ref[...]
    per_slot = 64 // n_coef
    for group in range(16):
        stack = []
        for b in range(4 * group, 4 * group + 4):
            lane = (b % per_slot) * 128
            stack.append(cg[b // per_slot, :, lane : lane + 128])
        stack = jnp.concatenate(stack, axis=0)
        kblocks[group] = dot(mix, jnp.concatenate([stack, stack], axis=1), (1, 1))
    for ks in order:
        for at, copy in dp_copies:
            if at == ks:
                copy.wait_recv()
        value = own_raw[ks]
        for kd in range(1, n_dp):
            value = value + raw_recv[ks, kd].astype(jnp.float32)
        if ks == 0:
            own_raw[0] = value
        else:
            z_send[ks] = value.astype(bf16)
            copy = send(
                z_send.at[ks], z_recv.at[ks], rs_sem.at[ks], rr_sem.at[ks],
                {"space": step(space, ks, n_space)},
            )
            copy.start()
            raw_copies.append(copy)
    for cycle in range(3):
        for half in range(2):
            source = []
            for q in range(4):
                start = (cycle * 8 + half * 4 + q) * 8
                part = kblocks[:, start : start + 8, :]
                source.append([rolled(part, s) for s in range(4)])
            fields = [
                lane_groups([source[q][(q - k) % 4] for q in range(4)], (16, 8, 128)) for k in range(4)
            ]
            value = jnp.stack(fields, axis=1).reshape(512, 128).astype(bf16)
            kt[cycle, :, half * 128 : (half + 1) * 128] = value

    wait_halo(m_down, m_up)
    lane = lax.broadcasted_iota(jnp.int32, (pix, 512), 1)
    low = lax.rem(lane, 8) < 2
    total = None
    for turn in (3, 2, 1, 0):
        if total is not None:
            total = jnp.where(low, pltpu.roll(total, 512 - 6, 1), pltpu.roll(total, 2, 1))
        for cycle in range(2):
            dr, dc = TURNS[cycle][turn]
            parts = [shifted(mp, 1 + r - dr, -dc) for r in range(rows)]
            value = turned(jnp.concatenate(parts, axis=0), turn)
            term = dot(value, kt[cycle + 1], (1, 1))
            total = term if total is None else total + term
    total = total + dot(own_m, kt[0], (1, 1))
    left, right = total[:, :256], total[:, 256:]
    is_first = chan == 0
    back_own[...] = jnp.where(is_first, left, right)
    back_send[...] = jnp.where(is_first, right, left).astype(bf16)
    back_copy = send(back_send, back_recv, bs_sem, br_sem, {"chan": 1 - chan})
    back_copy.start()

    conv = dot(xp[cols : pix + cols, :], kt[0], (1, 0))
    for turn in range(4):
        at = slice(turn * pix, (turn + 1) * pix)
        term = dot(xs[0, at, :], kt[1], (1, 0)) + dot(xs[1, at, :], kt[2], (1, 0))
        conv = conv + (pltpu.roll(term, 64 * turn, 1) if turn else term)
    for copy in raw_copies:
        copy.wait_recv()
    summed = own_raw[0]
    for ks in range(1, n_space):
        summed = summed + z_recv[ks].astype(jnp.float32)
    sq_send[...] = jnp.sum((summed * summed).reshape(per * 16, 8, 128), axis=0)
    sq_copies = []
    for k, peer in enumerate(peers):
        copy = send(sq_send, sq_recv.at[me_all], ss_sem.at[k], sr_sem.at[k], device(*peer))
        copy.start()
        sq_copies.append(copy)
    sq_recv[me_all] = sq_send[...]

    out_ref[...] = dot(conv.astype(bf16), to_rot, (1, 1)).astype(bf16)

    back_copy.wait_recv()
    back_ref[...] = (back_own[...] + back_recv[...].astype(jnp.float32)).astype(bf16)

    flipped = [summed[g].T for g in range(per)]
    for copy in sq_copies:
        copy.wait_recv()
    squares = jnp.sum(jnp.sum(sq_recv[...], axis=0), keepdims=True)
    factor = math.sqrt(FIELDS * FIELDS * 8 * NB) / jnp.sqrt(squares + 1e-06)
    for b in range(4 * per):
        grad_ref[:, b * 128 : (b + 1) * 128] = flipped[b // 4][(b % 4) * 32 : (b % 4 + 1) * 32, :] * factor

    @pl.when(space < n_space - 1)
    def _():
        x_down.wait_send()
        m_down.wait_send()

    @pl.when(space > 0)
    def _():
        x_up.wait_send()
        m_up.wait_send()

    for copy in coef_copies + [c for _, c in dp_copies] + raw_copies + sq_copies + [back_copy]:
        copy.wait_send()


def hand_on(a, b, c, a_out, b_out, c_out, a_mid, b_mid, c_mid, in_sem, out_sem):
    mids = (a_mid, b_mid, c_mid)
    loads = [pltpu.make_async_copy(src, mid, in_sem.at[k]) for k, (src, mid) in enumerate(zip((a, b, c), mids))]
    stores = [
        pltpu.make_async_copy(mid, dst, out_sem.at[k])
        for k, (mid, dst) in enumerate(zip(mids, (a_out, b_out, c_out)))
    ]
    for load in loads:
        load.start()
    for load, store in zip(loads, stores):
        load.wait()
        store.start()
    for store in stores:
        store.wait()


def fused(sizes, features, cotangent, valid, coefficients):
    n_space, n_dp, n_chan, rows, cols = sizes
    pix = rows * cols
    n_own, n_coef = n_space * n_dp, n_dp * n_chan
    n_all = n_own * n_chan
    per = 16 // n_own
    bf16, f32 = jnp.bfloat16, jnp.float32
    table = mixing_matrix()
    high = table.astype(bf16)
    low = (table - high.astype(np.float32)).astype(bf16)
    mix = jnp.asarray(np.concatenate([high, low], axis=1))
    mixt = jnp.asarray(np.ascontiguousarray(high.T))
    vmem = pl.BlockSpec(memory_space=pltpu.VMEM)
    dma = pltpu.SemaphoreType.DMA
    out, back, grad = pl.pallas_call(
        functools.partial(fused_kernel, sizes),
        out_shape=(
            jax.ShapeDtypeStruct((pix, 256), bf16),
            jax.ShapeDtypeStruct((pix, 256), bf16),
            jax.ShapeDtypeStruct((32, per * 512), f32),
        ),
        in_specs=[pl.BlockSpec(memory_space=pltpu.HBM)] * 6,
        out_specs=[vmem] * 3,
        scratch_shapes=[
            pltpu.VMEM((pix + 2 * cols, 512), bf16),
            pltpu.VMEM((pix + 2 * cols, 256), bf16),
            pltpu.VMEM((n_coef, 32, coefficients.shape[1]), bf16),
            pltpu.VMEM((2, 4 * pix, 512), bf16),
            pltpu.VMEM((16, 192, 128), f32),
            pltpu.VMEM((3, 512, 256), bf16),
            pltpu.VMEM((pix, 256), f32),
            pltpu.VMEM((pix, 256), bf16),
            pltpu.VMEM((pix, 256), bf16),
            pltpu.VMEM((n_space, n_dp, per, 128, 128), bf16),
            pltpu.VMEM((n_space, n_dp, per, 128, 128), bf16),
            pltpu.VMEM((8, 128), f32),
            pltpu.VMEM((n_all, 8, 128), f32),
            pltpu.VMEM((pix, 256), bf16),
            pltpu.VMEM((rows, cols), jnp.int32),
            pltpu.VMEM((32, coefficients.shape[1]), bf16),
            pltpu.VMEM(mix.shape, bf16),
            pltpu.VMEM(mixt.shape, bf16),
            dma((6,)),
            pltpu.VMEM((n_space, per, 128, 128), f32),
            pltpu.VMEM((n_space, per, 128, 128), bf16),
            pltpu.VMEM((n_space, per, 128, 128), bf16),
            pltpu.VMEM((16, 192, 128), f32),
            dma((n_space, n_dp)), dma((n_space, n_dp)),
            dma((4,)), dma((4,)),
            dma((n_coef,)), dma((n_coef,)),
            dma, dma,
            dma((n_space,)), dma((n_space,)),
            dma((n_all,)), dma((n_all,)),
        ],
        compiler_params=pltpu.CompilerParams(
            collective_id=0, has_side_effects=True, vmem_limit_bytes=63 * 1024 * 1024
        ),
    )(
        features.reshape(pix, 512),
        cotangent.reshape(pix, 256),
        valid.reshape(rows, cols),
        coefficients,
        mix,
        mixt,
    )
    hbm = pl.BlockSpec(memory_space=pltpu.HBM)
    out, back, grad = pl.pallas_call(
        hand_on,
        out_shape=tuple(jax.ShapeDtypeStruct(a.shape, a.dtype) for a in (out, back, grad)),
        in_specs=[hbm] * 3,
        out_specs=[hbm] * 3,
        scratch_shapes=[pltpu.VMEM(a.shape, a.dtype) for a in (out, back, grad)] + [dma((3,)), dma((3,))],
        compiler_params=pltpu.CompilerParams(vmem_limit_bytes=63 * 1024 * 1024),
    )(out, back, grad)
    shape = (1, rows, cols, 256)
    return out.reshape(shape), back.reshape(shape), grad


def block(features, cotangent, valid, coefficients):
    n_space, n_dp, n_chan = (lax.axis_size(a) for a in ("space", "dp", "chan"))
    cameras, rows, cols, _ = features.shape
    owners = n_space * n_dp
    if cameras == 1 and n_chan == 2 and owners <= 16 and 16 % owners == 0 and cols % 16 == 0 and owners > 1:
        sizes = (n_space, n_dp, n_chan, rows, cols)
        return fused(sizes, features, cotangent, valid, coefficients)
    return local(features, cotangent, valid, coefficients)


def solution(mesh):
    in_specs = (
        P(("parts", "dp"), "space", None, None),
        P(("parts", "dp"), "space", None, "chan"),
        P(("parts", "dp"), "space", None),
        P(None, ("dp", "chan")),
    )
    out_specs = (
        P(("parts", "dp"), "space", None, "chan"),
        P(("parts", "dp"), "space", None, "chan"),
        P(("parts", "chan"), ("space", "dp")),
    )
    return jax.shard_map(block, mesh=mesh, in_specs=in_specs, out_specs=out_specs, check_vma=False)
```
